32 devices in a mesh: groups: 2 (over x), pts: 16 (over z, y, core).
Axes of the slice: x: 2, y: 2, z: 4, core: 2. Of those that a mesh axis runs over, the one named last changes fastest.
Arguments:
- points: float32 [64, 131072], P(None, ('groups', 'pts')), parts along dimension 1, may hold values from -16 to 16
- right_side: float32 [16, 131072], P(None, ('groups', 'pts')), parts along dimension 1, may hold values from -24 to 24
- leaf_basis: float32 [512, 64, 256], P(('groups', 'pts')), parts along dimension 0, may hold values from -0.375 to 0.375
- local_transfer: float32 [960, 4096], P(('groups', 'pts')), parts along dimension 0, may hold values from -0.375 to 0.375
- local_skeleton: float32 [448, 4096], P(('groups', 'pts')), parts along dimension 0, may hold values from -16 to 16
- top_transfer: float32 [60, 4096], P('groups'), parts along dimension 0, may hold values from -0.375 to 0.375
- top_skeleton: float32 [60, 4096], P('groups'), parts along dimension 0, may hold values from -16 to 16
- node_slot: int32 [60], P('groups'), parts along dimension 0, may hold values from 0 to 29, each once
- near_leaves: int32 [512, 8], P(('groups', 'pts')), parts along dimension 0, may hold values from -1 to 255, as said below
Outputs:
- solution: float32 [16, 131072], P(None, ('groups', 'pts')), parts along dimension 1
- residual: float32 [16, 131072], P(None, ('groups', 'pts')), parts along dimension 1
The draws below stay inside these ranges and needn't reach their ends.
There are 2 independent parts, one for each index of `groups`. The reference program is written for one: setup_inputs(seed, part) draws one part's arguments, and reference() takes and returns one part's arrays. A program takes and returns all parts, laid end to end along the dimension named above; each array names one. Nothing has to cross between parts.
Inputs may be any that keep to these rules, and one draw needn't show every extreme that they name: `near_leaves`: every listed partner of leaf l is a distinct leaf m with l < m <= l + 16; a leaf's list holds min(8, number of such leaves) partners and -1 in the remaining places, so only the last leaves have padding.
All inputs are finite; a program needn't handle non-finite values.
Results may differ from the reference program's by a relative error of at most 0.0003.
Values sent between devices are 32-bit elements; how exact they have to be, the bound alone decides.
A program may use at most 192 MiB of HBM per device.

```python
import math
import jax
import jax.numpy as jnp
from jax import lax

DIM = 64
LEAF = 256
RANK = 64
NRHS = 16
NEAR = 8
ITERS = 3
LEAVES_DEV = 16
NLEAF = 256
NPOINTS = 65536
TOP_NODES = 30
LOCAL_NODES = 480
LOCAL_SKEL = 224
N_PTS = 16


def log_scales(key, shape, low, high):
    return jnp.exp(jax.random.uniform(key, shape, jnp.float32, jnp.log(low), jnp.log(high)))


def draw_points(key, part):
    key = jax.random.fold_in(key, 101)
    key_dir, key_scale = jax.random.split(key, 2)
    unit = jax.random.normal(key_dir, (DIM, NPOINTS), jnp.float32)
    return jnp.clip(unit * log_scales(key_scale, (1, NPOINTS), 1.0, 3.0), -16.0, 16.0)


def draw_right_side(key, part):
    key = jax.random.fold_in(key, 202)
    key_dir, key_scale = jax.random.split(key)
    rising = jnp.exp(jnp.log(3.0) * jnp.arange(NPOINTS, dtype=jnp.float32) / NPOINTS)[None, :]
    unit = jax.random.normal(key_dir, (NRHS, NPOINTS), jnp.float32)
    return jnp.clip(unit * rising * log_scales(key_scale, (1, NPOINTS), 0.5, 2.0), -24.0, 24.0)


def draw_local_skeleton(key, part):
    key = jax.random.fold_in(key, 303)
    key_dir, key_scale = jax.random.split(key)
    unit = jax.random.normal(key_dir, (LOCAL_SKEL, DIM, RANK), jnp.float32)
    values = unit * log_scales(key_scale, (LOCAL_SKEL, 1, RANK), 1.0, 3.0)
    return jnp.clip(values, -16.0, 16.0).reshape(LOCAL_SKEL, DIM * RANK)


def draw_top_skeleton(key, part):
    key = jax.random.fold_in(key, 404)
    key_dir, key_scale = jax.random.split(key)
    unit = jax.random.normal(key_dir, (TOP_NODES, DIM, RANK), jnp.float32)
    values = unit * log_scales(key_scale, (TOP_NODES, 1, RANK), 1.0, 3.0)
    return jnp.clip(values, -16.0, 16.0).reshape(TOP_NODES, DIM * RANK)


def draw_near_leaves(key, part):
    key = jax.random.fold_in(key, 505)
    offsets = jnp.arange(1, LEAVES_DEV + 1, dtype=jnp.int32)[None, :]
    leaf_ids = jnp.arange(NLEAF, dtype=jnp.int32)[:, None]
    targets = leaf_ids + offsets
    scores = jax.random.randint(key, (NLEAF, LEAVES_DEV), 0, 1 << 20, dtype=jnp.int32) * LEAVES_DEV + offsets - 1
    scores = jnp.where(targets < NLEAF, scores, scores + (1 << 20) * LEAVES_DEV)
    order = jnp.argsort(scores, axis=1, stable=True)[:, :NEAR]
    chosen = jnp.take_along_axis(targets, order, axis=1)
    return jnp.where(chosen < NLEAF, chosen, -1).astype(jnp.int32)


def level_of(key, extent, cuts, low, top_value):
    def one(axis_at, shards_of):
        heights = jax.random.uniform(jax.random.fold_in(jax.random.fold_in(key, 6), axis_at), (shards_of,), jnp.float32, low / len(cuts), top_value / len(cuts))
        return jnp.repeat(jnp.exp(heights), extent[axis_at] // shards_of).reshape((-1,) + (1,) * (len(extent) - axis_at - 1))

    factor_of = one(*cuts[0])
    for cut in cuts[1:]:
        factor_of = factor_of * one(*cut)
    return factor_of


def centred(stream_key, shape, scale, most, shards=(), kind=jnp.bfloat16):
    array = scale * jax.random.normal(stream_key, shape, jnp.float32)
    if shards:
        array = array * level_of(stream_key, shape, shards, -0.22, 0.18)
    return jnp.clip(array, -most, most).astype(kind)


def setup_inputs(seed: int = 0, part: int = 0) -> dict:
    arg_keys = jax.random.split(jax.random.key(seed), 10)
    part_keys = jax.random.split(jax.random.fold_in(arg_keys[9], part), 10)
    points = draw_points(jax.random.fold_in(jax.random.fold_in(arg_keys[9], part), 71), part)
    right_side = draw_right_side(jax.random.fold_in(jax.random.fold_in(arg_keys[9], part), 71), part)
    leaf_basis = centred(part_keys[2], (NLEAF, RANK, LEAF), LEAF ** -0.5, 0.375, ((0, 16),), jnp.float32)
    local_transfer = centred(part_keys[3], (LOCAL_NODES, RANK * RANK), (RANK * 4) ** -0.5, 0.375, ((0, 16),), jnp.float32)
    local_skeleton = draw_local_skeleton(jax.random.fold_in(jax.random.fold_in(arg_keys[9], part), 71), part)
    top_transfer = centred(part_keys[5], (TOP_NODES, RANK * RANK), (RANK * 4) ** -0.5, 0.375, (), jnp.float32)
    top_skeleton = draw_top_skeleton(jax.random.fold_in(jax.random.fold_in(arg_keys[9], part), 71), part)
    node_slot = jax.random.permutation(part_keys[7], TOP_NODES).astype(jnp.int32)
    near_leaves = draw_near_leaves(jax.random.fold_in(jax.random.fold_in(arg_keys[9], part), 71), part)
    return dict(points=points, right_side=right_side, leaf_basis=leaf_basis, local_transfer=local_transfer, local_skeleton=local_skeleton, top_transfer=top_transfer, top_skeleton=top_skeleton, node_slot=node_slot, near_leaves=near_leaves)


RIDGE = 8.0
HIGH = lax.Precision.HIGHEST

def kernel_block(left, right):
    features = left.shape[-2]
    left_sq = lax.optimization_barrier(jnp.sum(left * left, axis=-2))[..., :, None]
    right_sq = lax.optimization_barrier(jnp.sum(right * right, axis=-2))[..., None, :]
    cross = jnp.einsum('...dn,...dm->...nm', left, right, precision=HIGH)
    return jnp.exp((2.0 * cross - left_sq - right_sq) / (2.0 * features))

def couple_pairs(blocks, charges):
    pairs = blocks.shape[0]
    paired = charges.reshape(pairs, 2, charges.shape[1], charges.shape[2])
    first = jnp.einsum('prs,pns->pnr', blocks, paired[:, 1], precision=HIGH)
    second = jnp.einsum('prs,pnr->pns', blocks, paired[:, 0], precision=HIGH)
    return jnp.stack([first, second], axis=1).reshape(charges.shape)

def lift_charges(charges, transfer):
    lifted = jnp.einsum('jnc,jcp->jnp', charges, transfer, precision=HIGH)
    return lifted.reshape(-1, 2, lifted.shape[1], lifted.shape[2]).sum(axis=1)

def lower_potential(potential, transfer):
    return jnp.einsum('jnp,jcp->jnc', jnp.repeat(potential, 2, axis=0), transfer, precision=HIGH)

def level_tables(local_transfer, local_skeleton, top_transfer, top_skeleton, node_slot):
    low_depths = LEAVES_DEV.bit_length() - 1
    top_depths = N_PTS.bit_length() - 1
    coupling = 1.0 / math.sqrt(RANK)
    lower_e = local_transfer.reshape(N_PTS, 2 * LEAVES_DEV - 2, RANK, RANK)
    lower_s = local_skeleton.reshape(N_PTS, LEAVES_DEV - 2, DIM, RANK)
    transfers = []
    pair_blocks = [None]
    for depth in range(low_depths):
        node_count = LEAVES_DEV >> depth
        offset = 2 * LEAVES_DEV - 2 * node_count
        transfers.append(lower_e[:, offset:offset + node_count].reshape(N_PTS * node_count, RANK, RANK))
        if depth > 0:
            first_row = LEAVES_DEV - (LEAVES_DEV >> depth - 1)
            skeletons = lower_s[:, first_row:first_row + node_count].reshape(N_PTS * node_count // 2, 2, DIM, RANK)
            pair_blocks.append(kernel_block(skeletons[:, 0], skeletons[:, 1]) * coupling)
    for depth in range(top_depths):
        node_count = N_PTS >> depth
        offset = 2 * N_PTS - 2 * node_count
        slots = node_slot[offset:offset + node_count]
        transfers.append(top_transfer[slots].reshape(node_count, RANK, RANK))
        skeletons = top_skeleton[slots].reshape(node_count // 2, 2, DIM, RANK)
        pair_blocks.append(kernel_block(skeletons[:, 0], skeletons[:, 1]) * coupling)
    return (transfers, pair_blocks)

def far_field(vec, leaf_basis, transfers, pair_blocks):
    depth_total = len(transfers)
    blocks = vec.reshape(NRHS, NLEAF, LEAF)
    charges = [jnp.einsum('lrp,nlp->lnr', leaf_basis, blocks, precision=HIGH)]
    for depth in range(depth_total - 1):
        charges.append(lift_charges(charges[-1], transfers[depth]))
    potential = couple_pairs(pair_blocks[depth_total - 1], charges[depth_total - 1])
    for depth in range(depth_total - 2, -1, -1):
        potential = lower_potential(potential, transfers[depth])
        if depth > 0:
            potential = potential + couple_pairs(pair_blocks[depth], charges[depth])
    result = jnp.einsum('lrp,lnr->nlp', leaf_basis, potential, precision=HIGH)
    return result.reshape(NRHS, NPOINTS)

def near_field(vec, points, near_leaves):
    scale = 1.0 / math.sqrt(LEAF)
    leaf_points = points.reshape(DIM, NLEAF, LEAF).transpose(1, 0, 2)
    leaf_values = vec.reshape(NRHS, NLEAF, LEAF).transpose(1, 0, 2)
    present = (near_leaves >= 0).astype(jnp.float32)
    partner = jnp.where(near_leaves >= 0, near_leaves, 0).astype(jnp.int32)

    def one_device(pieces):
        own_points, own_values, partner_ids, weights = pieces
        self_blocks = kernel_block(own_points, own_points) * scale
        cross_blocks = kernel_block(own_points[:, None], leaf_points[partner_ids]) * scale
        partner_values = leaf_values[partner_ids] * weights[:, :, None, None]
        local_term = jnp.einsum('lim,lnm->lni', self_blocks, own_values, precision=HIGH)
        local_term = local_term + jnp.einsum('lkim,lknm->lni', cross_blocks, partner_values, precision=HIGH)
        sent = jnp.einsum('lkim,lni->lknm', cross_blocks, own_values, precision=HIGH) * weights[:, :, None, None]
        return (local_term, sent)
    local_term, sent = lax.map(one_device, (leaf_points.reshape(N_PTS, LEAVES_DEV, DIM, LEAF), leaf_values.reshape(N_PTS, LEAVES_DEV, NRHS, LEAF), partner.reshape(N_PTS, LEAVES_DEV, NEAR), present.reshape(N_PTS, LEAVES_DEV, NEAR)))
    total = local_term.reshape(NLEAF, NRHS, LEAF)
    total = total.at[partner.reshape(-1)].add(sent.reshape(NLEAF * NEAR, NRHS, LEAF))
    return total.transpose(1, 0, 2).reshape(NRHS, NPOINTS)

def reference(points, right_side, leaf_basis, local_transfer, local_skeleton, top_transfer, top_skeleton, node_slot, near_leaves):
    transfers, pair_blocks = level_tables(local_transfer, local_skeleton, top_transfer, top_skeleton, node_slot)

    def operate(vec):
        return RIDGE * vec + near_field(vec, points, near_leaves) + far_field(vec, leaf_basis, transfers, pair_blocks)
    solution = jnp.zeros_like(right_side)
    residual = right_side
    direction = right_side
    norm_now = lax.optimization_barrier(jnp.sum(residual * residual, axis=1))
    for sweep in range(ITERS):
        image = operate(direction)
        step_length = norm_now / lax.optimization_barrier(jnp.sum(direction * image, axis=1))
        solution = solution + step_length[:, None] * direction
        residual = residual - step_length[:, None] * image
        norm_next = lax.optimization_barrier(jnp.sum(residual * residual, axis=1))
        direction = residual + (norm_next / norm_now)[:, None] * direction
        norm_now = norm_next
    return (solution, residual)
```

```python
import functools
import math

import jax
import jax.numpy as jnp
from jax import lax
from jax.experimental import pallas as pl
from jax.experimental.pallas import tpu as pltpu
from jax.sharding import PartitionSpec as P

ITERS = 3
RIDGE = 8.0
HIGH = lax.Precision.HIGHEST
F32 = jnp.float32
BF16 = jnp.bfloat16


def dot_nn(a, b, precision=None):
    return lax.dot_general(
        a, b, (((1,), (0,)), ((), ())), precision=precision, preferred_element_type=F32
    )


def dot_nt(a, b, precision=None):
    return lax.dot_general(
        a, b, (((1,), (1,)), ((), ())), precision=precision, preferred_element_type=F32
    )


def split2(x):
    hi = x.astype(BF16)
    return hi, (x - hi.astype(F32)).astype(BF16)


def split3(x):
    hi = x.astype(BF16)
    rest = x - hi.astype(F32)
    mid = rest.astype(BF16)
    return hi, mid, (rest - mid.astype(F32)).astype(BF16)


def kernel_block(left, right, scale):
    features = left.shape[0]
    left_t = left.T
    left_sq = jnp.sum(left_t * left_t, axis=1, keepdims=True)
    right_sq = jnp.sum(right * right, axis=0, keepdims=True)
    cross = dot_nn(left_t, right, HIGH)
    return jnp.exp((2.0 * cross - left_sq - right_sq) * (0.5 / features)) * scale


def flipped(value, mask, bits):
    for bit in range(bits):
        weight = 1 << bit
        has = (mask // weight) % 2
        value = value + has * weight * (1 - 2 * ((value // weight) % 2))
    return value


def tree_kernel(
    devices, leaves, rank, slot_ref, le_ref, ls_ref, te_ref, ts_ref, mh_ref, ml_ref, r_ref, t_ref, u_ref
):
    me = lax.axis_index("pts")
    scale = 1.0 / math.sqrt(rank)
    low = leaves.bit_length() - 1
    top = devices.bit_length() - 1
    mh_ref[...] = jnp.zeros_like(mh_ref)
    ml_ref[...] = jnp.zeros_like(ml_ref)

    def local_e(row):
        return le_ref[row * rank : (row + 1) * rank, :]

    def local_s(row):
        return ls_ref[row * rank : (row + 1) * rank, :]

    u_ref[...] = le_ref[0 : leaves * rank, :]
    for depth in range(1, low + 1):
        count = leaves >> depth
        size = (1 << depth) * rank
        if depth < low:
            first = leaves - (leaves >> depth - 1)
            for pair in range(count // 2):
                b = kernel_block(local_s(first + 2 * pair), local_s(first + 2 * pair + 1), scale)
                a0, a1 = 2 * pair * size, (2 * pair + 1) * size
                x, y = u_ref[a0 : a0 + size, :], u_ref[a1 : a1 + size, :]
                p = dot_nn(x, b, HIGH)
                for rows, cols, block in (
                    (a0, a1, dot_nt(p, y, HIGH)),
                    (a1, a0, dot_nt(y, p, HIGH)),
                ):
                    hi, lo = split2(block)
                    mh_ref[rows : rows + size, cols : cols + size] = hi
                    ml_ref[rows : rows + size, cols : cols + size] = lo
            offset = 2 * leaves - 2 * count
            for node in range(count):
                rows = slice(node * size, (node + 1) * size)
                u_ref[rows, :] = dot_nn(u_ref[rows, :], local_e(offset + node), HIGH)
    r_ref[...] = u_ref[...]

    t_ref[...] = jnp.zeros_like(t_ref)

    def slot_of(depth, node):
        return slot_ref[2 * devices - 2 * (devices >> depth) + node]

    def top_row(ref, slot):
        return ref[pl.ds(pl.multiple_of(slot * rank, rank), rank), :]

    chain = None
    seeds = []
    for depth in range(top):
        mine = me // (1 << depth)
        own = slot_of(depth, mine)
        other = slot_of(depth, flipped(mine, 1, 1))
        b = kernel_block(top_row(ts_ref, other), top_row(ts_ref, own), scale)
        seeds.append(b if chain is None else dot_nt(b, chain, HIGH))
        e = top_row(te_ref, own)
        chain = e if chain is None else dot_nn(chain, e, HIGH)
    for depth in range(top - 1, -1, -1):
        mine = me // (1 << depth)
        count = devices >> depth

        def child(step, carry, depth=depth, mine=mine, count=count):
            x = count - 1 - step
            e = top_row(te_ref, slot_of(depth, flipped(mine, x, top - depth)))
            t_ref[x] = dot_nn(e, t_ref[x // 2], HIGH)
            return carry

        if count > 2:
            lax.fori_loop(0, count - 2, child, 0)
        t_ref[1] = seeds[depth]


def main_kernel(
    devices,
    leaves,
    rank,
    columns,
    leaf_size,
    features,
    slots,
    idx_ref,
    wt_ref,
    inv_ref,
    pts_ref,
    next_pts_ref,
    rhs_ref,
    next_rhs_ref,
    basis_ref,
    mh_ref,
    ml_ref,
    r_ref,
    t_ref,
    sol_ref,
    out_ref,
    kh,
    kl,
    bj,
    bd,
    vb,
    sent,
    res,
    along,
    dirn,
    img,
    halo_res,
    halo_along,
    halo_img,
    owed_out,
    owed_in,
    gather,
    g_send,
    g_recv,
    h_send,
    h_recv,
    o_send,
    o_recv,
):
    me = lax.axis_index("pts")
    bits = devices.bit_length() - 1
    following = (me + 1) % devices
    previous = (me + devices - 1) % devices
    near = slots - 1
    n = leaf_size
    barrier = pltpu.get_barrier_semaphore()

    def greet(d, carry):
        pl.semaphore_signal(
            barrier, inc=1, device_id={"pts": (me + d) % devices},
            device_id_type=pl.DeviceIdType.MESH,
        )
        return carry

    lax.fori_loop(1, devices, greet, 0)
    pl.semaphore_wait(barrier, devices - 1)

    def broadcast(slot):
        def post(d, carry):
            pltpu.make_async_remote_copy(
                src_ref=gather.at[slot, me],
                dst_ref=gather.at[slot, me],
                send_sem=g_send.at[slot],
                recv_sem=g_recv.at[slot],
                device_id={"pts": (me + d) % devices},
                device_id_type=pl.DeviceIdType.MESH,
            ).start()
            return carry

        lax.fori_loop(1, devices, post, 0)

    def collect(slot):
        others = gather.at[slot, pl.ds(0, devices - 1)]
        pltpu.make_async_copy(others, others, g_recv.at[slot]).wait()
        pltpu.make_async_copy(others, others, g_send.at[slot]).wait()

    def pair_of(ref, p):
        return jnp.concatenate([ref[2 * p], ref[2 * p + 1]], axis=1)

    def charges_of(ref):
        parts = [dot_nt(pair_of(ref, p), bd[p], HIGH) for p in range(leaves // 2)]
        return jnp.concatenate(parts, axis=1)

    def row_sum(first, second):
        total = first[0] * second[0]
        for l in range(1, leaves):
            total = total + first[l] * second[l]
        return jnp.sum(total, axis=1, keepdims=True)

    def post_message(slot, root, norm, product):
        half = (128 - rank) // 2
        gather[slot, me, :, 0:rank] = root
        gather[slot, me, :, rank : rank + half] = jnp.broadcast_to(norm, (columns, half))
        gather[slot, me, :, rank + half : 128] = jnp.broadcast_to(product, (columns, half))
        broadcast(slot)

    def sums_of(slot):
        total = gather[slot, 0]
        for d in range(1, devices):
            total = total + gather[slot, d]
        half = (128 - rank) // 2
        return total[:, rank : rank + 1], total[:, rank + half : rank + half + 1]

    def potential_of(slot):
        def add(x, total):
            d = flipped(me, x, bits)
            return total + dot_nn(gather[slot, d][:, 0:rank], t_ref[x], HIGH)

        return lax.fori_loop(1, devices, add, jnp.zeros((columns, rank), F32))

    bd[...] = jnp.zeros_like(bd)
    for l in range(leaves):
        odd = l % 2
        bd[l // 2, odd * rank : (odd + 1) * rank, odd * n : (odd + 1) * n] = basis_ref[l]
        res[l] = rhs_ref[:, l * n : (l + 1) * n]
        halo_res[l] = next_rhs_ref[:, l * n : (l + 1) * n]
    charge = charges_of(res)
    norm_local = row_sum(res, res)
    post_message(0, dot_nn(charge, r_ref[...], HIGH), norm_local, norm_local)

    sent[leaves * near] = jnp.zeros((columns, n), F32)

    def stack_right(x, row):
        hi, mid, lo = split3(x)
        nh, nm, nl = split3(-0.5 * jnp.sum(x * x, axis=0, keepdims=True))
        at = lax.broadcasted_iota(jnp.int32, (features, n), 0)
        extra = jnp.where(at < 3, 1.0, 0.0)
        for place, part in ((3, nh), (4, nm), (5, nl)):
            extra = jnp.where(at == place, part.astype(F32), extra)
        bj[row, 0:features, :] = hi
        bj[row, features : 2 * features, :] = mid
        bj[row, 2 * features : 3 * features, :] = lo
        bj[row, 3 * features : 4 * features, :] = extra.astype(BF16)

    def prepare(l, carry):
        at = pl.ds(pl.multiple_of(l * n, n), n)
        stack_right(pts_ref[:, at], l)
        stack_right(next_pts_ref[:, at], leaves + l)
        return carry

    lax.fori_loop(0, leaves, prepare, 0)

    def build(l, carry):
        x = pts_ref[:, pl.ds(pl.multiple_of(l * n, n), n)].T
        hi, mid, lo = split3(x)
        nh, nm, nl = split3(-0.5 * jnp.sum(x * x, axis=1, keepdims=True))
        at = lax.broadcasted_iota(jnp.int32, (n, features), 1)
        extra = jnp.where((at >= 3) & (at < 6), 1.0, 0.0)
        for place, part in ((0, nh), (1, nm), (2, nl)):
            extra = jnp.where(at == place, part.astype(F32), extra)
        left = jnp.concatenate([hi, hi, mid, mid, hi, lo, extra.astype(BF16)], axis=1)
        for k in range(slots):
            m = idx_ref[l * slots + k]
            rh = bj[m, 0:features, :]
            rm = bj[m, features : 2 * features, :]
            rl = bj[m, 2 * features : 3 * features, :]
            rx = bj[m, 3 * features : 4 * features, :]
            right = jnp.concatenate([rh, rm, rh, rm, rl, rh, rx], axis=0)
            block = jnp.exp(dot_nn(left, right) * (1.0 / features)) * wt_ref[l * slots + k]
            hi_part, lo_part = split2(block)
            kh[l * slots + k] = hi_part
            kl[l * slots + k] = lo_part
        return carry

    lax.fori_loop(0, leaves, build, 0)

    collect(0)
    potential = potential_of(0)
    step = norm_now = None
    charge_along = potential_along = None

    for sweep in range(ITERS):
        last = sweep + 1 == ITERS

        def load_field(l, carry):
            vb[l, 0:columns, :], vb[l, columns : 2 * columns, :] = split2(res[l])
            vb[leaves + l, 0:columns, :], vb[leaves + l, columns : 2 * columns, :] = split2(
                halo_res[l]
            )
            return carry

        lax.fori_loop(0, leaves, load_field, 0)

        def transposed(l, carry):
            both = vb[l]
            high = both[0:columns]
            for k in range(near):
                first = dot_nn(both, kh[l * slots + k])
                second = dot_nn(high, kl[l * slots + k])
                sent[l * near + k] = first[0:columns] + first[columns:] + second
            return carry

        lax.fori_loop(0, leaves, transposed, 0)

        for c in range(leaves):
            own = jnp.zeros((columns, n), F32)
            beyond = jnp.zeros((columns, n), F32)
            for l in range(leaves):
                term = sent[inv_ref[l * leaves + c]]
                if l < c:
                    own = own + term
                else:
                    beyond = beyond + term
            img[c] = own + RIDGE * res[c]
            owed_out[c] = beyond
        owed = pltpu.make_async_remote_copy(
            src_ref=owed_out,
            dst_ref=owed_in,
            send_sem=o_send.at[sweep],
            recv_sem=o_recv.at[sweep],
            device_id={"pts": following},
            device_id_type=pl.DeviceIdType.MESH,
        )
        owed.start()

        def forward(l, carry):
            total = jnp.zeros((2 * columns, n), F32)
            low = jnp.zeros((columns, n), F32)
            for k in range(slots):
                both = vb[idx_ref[l * slots + k]]
                total = total + dot_nt(both, kh[l * slots + k])
                low = low + dot_nt(both[0:columns], kl[l * slots + k])
            img[l] = img[l] + (total[0:columns] + total[columns:] + low)
            return carry

        lax.fori_loop(0, leaves, forward, 0)

        chi, clo = split2(charge)
        stacked = jnp.concatenate([chi, clo], axis=0)
        first = dot_nn(stacked, mh_ref[...])
        leaf_potential = first[0:columns] + first[columns:] + dot_nn(chi, ml_ref[...])
        leaf_potential = leaf_potential + dot_nt(potential, r_ref[...], HIGH)
        for p in range(leaves // 2):
            far = dot_nn(leaf_potential[:, 2 * p * rank : 2 * (p + 1) * rank], bd[p], HIGH)
            img[2 * p] = img[2 * p] + far[:, 0:n]
            img[2 * p + 1] = img[2 * p + 1] + far[:, n:]

        owed.wait()
        for l in range(leaves):
            img[l] = img[l] + owed_in[l]

        slot = (sweep + 1) % 2
        halo = None
        norm_local = row_sum(res, res)
        product_local = row_sum(res, img)
        if last:
            charge_img = None
            root = jnp.zeros((columns, rank), F32)
        else:
            halo = pltpu.make_async_remote_copy(
                src_ref=img,
                dst_ref=halo_img.at[sweep],
                send_sem=h_send.at[sweep],
                recv_sem=h_recv.at[sweep],
                device_id={"pts": previous},
                device_id_type=pl.DeviceIdType.MESH,
            )
            halo.start()
            charge_img = charges_of(img)
            root = dot_nn(charge_img, r_ref[...], HIGH)
        post_message(slot, root, norm_local, product_local)
        if not last:
            halo.wait()
        collect(slot)
        norm_next, product = sums_of(slot)
        if sweep == 0:
            step = norm_next / product
        else:
            ratio = norm_next / norm_now
            step = norm_next / (product - ratio * norm_next / step)
        norm_now = norm_next
        if not last:
            potential_img = potential_of(slot)
            if sweep == 0:
                charge_along, potential_along = charge_img, potential_img
            else:
                charge_along = charge_img + ratio * charge_along
                potential_along = potential_img + ratio * potential_along
            charge = charge - step * charge_along
            potential = potential - step * potential_along
        for l in range(leaves):
            at = slice(l * n, (l + 1) * n)
            if sweep == 0:
                d, a = res[l], img[l]
                sol = step * d
            else:
                d = res[l] + ratio * dirn[l]
                a = img[l] + ratio * along[l]
                sol = sol_ref[:, at] + step * d
            sol_ref[:, at] = sol
            r = res[l] - step * a
            if last:
                out_ref[:, at] = r
                continue
            dirn[l], along[l], res[l] = d, a, r
            a = halo_img[sweep, l]
            if sweep > 0:
                a = a + ratio * halo_along[l]
            halo_along[l] = a
            halo_res[l] = halo_res[l] - step * a


def per_device(
    points,
    right_side,
    leaf_basis,
    local_transfer,
    local_skeleton,
    top_transfer,
    top_skeleton,
    node_slot,
    near_leaves,
):
    features = points.shape[0]
    leaves, rank, leaf_size = leaf_basis.shape
    columns = right_side.shape[0]
    near = near_leaves.shape[1]
    slots = near + 1
    devices = lax.axis_size("pts")
    position = lax.axis_index("pts")
    ring = [(source, (source - 1) % devices) for source in range(devices)]
    next_rhs = lax.ppermute(right_side, "pts", ring)
    next_points = lax.ppermute(points, "pts", ring)

    present = near_leaves >= 0
    partner = jnp.where(present, near_leaves - position * leaves, -1)
    ids = jnp.arange(leaves, dtype=jnp.int32)
    index = jnp.concatenate([jnp.maximum(partner, 0), ids[:, None]], axis=1).reshape(-1)
    scale = 1.0 / math.sqrt(leaf_size)
    weight = jnp.concatenate([present, jnp.ones((leaves, 1), bool)], axis=1)
    weight = (weight.astype(F32) * scale).reshape(-1)
    target = jnp.where(ids[:, None] < ids[None, :], ids[None, :], ids[None, :] + leaves)
    match = partner[:, None, :] == target[:, :, None]
    place = ids[:, None] * near + jnp.arange(near, dtype=jnp.int32)[None, :]
    inverse = jnp.min(jnp.where(match, place[:, None, :], leaves * near), axis=2).reshape(-1)

    vmem = pl.BlockSpec(memory_space=pltpu.VMEM)
    smem = pl.BlockSpec(memory_space=pltpu.SMEM)
    inner = leaves * rank
    mh, ml, r, t = pl.pallas_call(
        functools.partial(tree_kernel, devices, leaves, rank),
        out_shape=(
            jax.ShapeDtypeStruct((inner, inner), BF16),
            jax.ShapeDtypeStruct((inner, inner), BF16),
            jax.ShapeDtypeStruct((inner, rank), F32),
            jax.ShapeDtypeStruct((devices, rank, rank), F32),
        ),
        in_specs=[smem] + [vmem] * 4,
        out_specs=(vmem,) * 4,
        scratch_shapes=[pltpu.VMEM((inner, rank), F32)],
        compiler_params=pltpu.CompilerParams(vmem_limit_bytes=48 * 1024 * 1024),
        cost_estimate=pl.CostEstimate(
            flops=20_000_000_000, bytes_accessed=20_000_000, transcendentals=0
        ),
        name="tree",
    )(
        node_slot,
        local_transfer.reshape(-1, rank),
        local_skeleton.reshape(-1, rank),
        top_transfer.reshape(-1, rank),
        top_skeleton.reshape(-1, rank),
    )

    field = (leaves, columns, leaf_size)
    width = leaves * leaf_size
    return pl.pallas_call(
        functools.partial(
            main_kernel, devices, leaves, rank, columns, leaf_size, features, slots
        ),
        out_shape=(jax.ShapeDtypeStruct((columns, width), F32),) * 2,
        in_specs=[smem] * 3 + [vmem] * 9,
        out_specs=(vmem,) * 2,
        scratch_shapes=[
            pltpu.VMEM((leaves * slots, leaf_size, leaf_size), BF16),
            pltpu.VMEM((leaves * slots, leaf_size, leaf_size), BF16),
            pltpu.VMEM((2 * leaves, 4 * features, leaf_size), BF16),
            pltpu.VMEM((leaves // 2, 2 * rank, 2 * leaf_size), F32),
            pltpu.VMEM((2 * leaves, 2 * columns, leaf_size), BF16),
            pltpu.VMEM((leaves * near + 1, columns, leaf_size), F32),
            pltpu.VMEM(field, F32),
            pltpu.VMEM(field, F32),
            pltpu.VMEM(field, F32),
            pltpu.VMEM(field, F32),
            pltpu.VMEM(field, F32),
            pltpu.VMEM(field, F32),
            pltpu.VMEM((ITERS - 1,) + field, F32),
            pltpu.VMEM(field, F32),
            pltpu.VMEM(field, F32),
            pltpu.VMEM((2, devices, columns, 128), F32),
            pltpu.SemaphoreType.DMA((2,)),
            pltpu.SemaphoreType.DMA((2,)),
            pltpu.SemaphoreType.DMA((ITERS,)),
            pltpu.SemaphoreType.DMA((ITERS,)),
            pltpu.SemaphoreType.DMA((ITERS,)),
            pltpu.SemaphoreType.DMA((ITERS,)),
        ],
        compiler_params=pltpu.CompilerParams(
            collective_id=0, has_side_effects=True, vmem_limit_bytes=66 * 1000 * 1000
        ),
        name="gradients",
    )(index, weight, inverse, points, next_points, right_side, next_rhs, leaf_basis, mh, ml, r, t)


def solution(mesh):
    return jax.shard_map(
        per_device,
        mesh=mesh,
        in_specs=(
            P(None, ("groups", "pts")),
            P(None, ("groups", "pts")),
            P(("groups", "pts"), None, None),
            P(("groups", "pts"), None),
            P(("groups", "pts"), None),
            P("groups", None),
            P("groups", None),
            P("groups"),
            P(("groups", "pts"), None),
        ),
        out_specs=(P(None, ("groups", "pts")), P(None, ("groups", "pts"))),
        check_vma=False,
    )
```

```python
import functools
import math

import jax
import jax.numpy as jnp
from jax import lax
from jax.experimental import pallas as pl
from jax.experimental.pallas import tpu as pltpu
from jax.sharding import PartitionSpec as P

ITERS = 3
RIDGE = 8.0
HIGH = lax.Precision.HIGHEST
F32 = jnp.float32
BF16 = jnp.bfloat16


def dot_nn(a, b, precision=None):
    return lax.dot_general(
        a, b, (((1,), (0,)), ((), ())), precision=precision, preferred_element_type=F32
    )


def dot_nt(a, b, precision=None):
    return lax.dot_general(
        a, b, (((1,), (1,)), ((), ())), precision=precision, preferred_element_type=F32
    )


def split2(x):
    hi = x.astype(BF16)
    return hi, (x - hi.astype(F32)).astype(BF16)


def split3(x):
    hi = x.astype(BF16)
    rest = x - hi.astype(F32)
    mid = rest.astype(BF16)
    return hi, mid, (rest - mid.astype(F32)).astype(BF16)


def split_dot(dot, x, hi, lo):
    rows = x.shape[0]
    xh, xl = split2(x)
    first = dot(jnp.concatenate([xh, xl], axis=0), hi)
    return first[0:rows] + first[rows:] + dot(xh, lo)


def kernel_block(left, right, scale):
    features = left.shape[0]
    left_t = left.T
    left_sq = jnp.sum(left_t * left_t, axis=1, keepdims=True)
    right_sq = jnp.sum(right * right, axis=0, keepdims=True)
    cross = dot_nn(left_t, right, HIGH)
    return jnp.exp((2.0 * cross - left_sq - right_sq) * (0.5 / features)) * scale


def flipped(value, mask, bits):
    for bit in range(bits):
        weight = 1 << bit
        has = (mask // weight) % 2
        value = value + has * weight * (1 - 2 * ((value // weight) % 2))
    return value


def tree_kernel(
    devices, leaves, rank, slot_ref, le_ref, ls_ref, te_ref, ts_ref, mh_ref, ml_ref, rh_ref, rl_ref, t_ref, u_ref
):
    me = lax.axis_index("pts")
    scale = 1.0 / math.sqrt(rank)
    low = leaves.bit_length() - 1
    top = devices.bit_length() - 1
    mh_ref[...] = jnp.zeros_like(mh_ref)
    ml_ref[...] = jnp.zeros_like(ml_ref)

    def local_e(row):
        return le_ref[row * rank : (row + 1) * rank, :]

    def local_s(row):
        return ls_ref[row * rank : (row + 1) * rank, :]

    u_ref[...] = le_ref[0 : leaves * rank, :]
    for depth in range(1, low + 1):
        count = leaves >> depth
        size = (1 << depth) * rank
        if depth < low:
            first = leaves - (leaves >> depth - 1)
            for pair in range(count // 2):
                b = kernel_block(local_s(first + 2 * pair), local_s(first + 2 * pair + 1), scale)
                a0, a1 = 2 * pair * size, (2 * pair + 1) * size
                x, y = u_ref[a0 : a0 + size, :], u_ref[a1 : a1 + size, :]
                p = dot_nn(x, b, HIGH)
                for rows, cols, block in (
                    (a0, a1, dot_nt(p, y, HIGH)),
                    (a1, a0, dot_nt(y, p, HIGH)),
                ):
                    hi, lo = split2(block)
                    mh_ref[rows : rows + size, cols : cols + size] = hi
                    ml_ref[rows : rows + size, cols : cols + size] = lo
            offset = 2 * leaves - 2 * count
            for node in range(count):
                rows = slice(node * size, (node + 1) * size)
                u_ref[rows, :] = dot_nn(u_ref[rows, :], local_e(offset + node), HIGH)
    rh_ref[...], rl_ref[...] = split2(u_ref[...])

    t_ref[...] = jnp.zeros_like(t_ref)

    def slot_of(depth, node):
        return slot_ref[2 * devices - 2 * (devices >> depth) + node]

    def top_row(ref, slot):
        return ref[pl.ds(pl.multiple_of(slot * rank, rank), rank), :]

    chain = None
    seeds = []
    for depth in range(top):
        mine = me // (1 << depth)
        own = slot_of(depth, mine)
        other = slot_of(depth, flipped(mine, 1, 1))
        b = kernel_block(top_row(ts_ref, other), top_row(ts_ref, own), scale)
        seeds.append(b if chain is None else dot_nt(b, chain, HIGH))
        e = top_row(te_ref, own)
        chain = e if chain is None else dot_nn(chain, e, HIGH)
    for depth in range(top - 1, -1, -1):
        mine = me // (1 << depth)
        count = devices >> depth

        group = min(count, 16)

        def family(step, carry, depth=depth, mine=mine, count=count, group=group):
            base = count - (step + 1) * group
            parents = [t_ref[(base + i) // 2] for i in range(group)]
            for i in range(group):
                e = top_row(te_ref, slot_of(depth, flipped(mine, base + i, top - depth)))
                t_ref[base + i] = dot_nn(e, parents[i], HIGH)
            return carry

        if count > 2:
            lax.fori_loop(0, count // group, family, 0)
        t_ref[1] = seeds[depth]


def main_kernel(
    devices,
    leaves,
    rank,
    columns,
    leaf_size,
    features,
    slots,
    idx_ref,
    wt_ref,
    inv_ref,
    pts_ref,
    next_pts_ref,
    rhs_ref,
    next_rhs_ref,
    basis_ref,
    mh_ref,
    ml_ref,
    rh_ref,
    rl_ref,
    t_ref,
    sol_ref,
    out_ref,
    kh,
    kl,
    bj,
    bdh,
    bdl,
    vb,
    sent,
    res,
    along,
    dirn,
    img,
    w,
    second_along,
    halo_in,
    owed_out,
    owed_in,
    gather,
    g_send,
    g_recv,
    h_send,
    h_recv,
    o_send,
    o_recv,
):
    me = lax.axis_index("pts")
    bits = devices.bit_length() - 1
    following = (me + 1) % devices
    previous = (me + devices - 1) % devices
    near = slots - 1
    n = leaf_size
    barrier = pltpu.get_barrier_semaphore()

    def greet(d, carry):
        pl.semaphore_signal(
            barrier, inc=1, device_id={"pts": (me + d) % devices},
            device_id_type=pl.DeviceIdType.MESH,
        )
        return carry

    lax.fori_loop(1, devices, greet, 0)
    pl.semaphore_wait(barrier, devices - 1)

    def broadcast(slot):
        def post(d, carry):
            pltpu.make_async_remote_copy(
                src_ref=gather.at[slot, me],
                dst_ref=gather.at[slot, me],
                send_sem=g_send.at[slot],
                recv_sem=g_recv.at[slot],
                device_id={"pts": (me + d) % devices},
                device_id_type=pl.DeviceIdType.MESH,
            ).start()
            return carry

        lax.fori_loop(1, devices, post, 0)

    def collect(slot):
        others = gather.at[slot, pl.ds(0, devices - 1)]
        pltpu.make_async_copy(others, others, g_recv.at[slot]).wait()
        pltpu.make_async_copy(others, others, g_send.at[slot]).wait()

    def pair_of(ref, p):
        return jnp.concatenate([ref[2 * p], ref[2 * p + 1]], axis=1)

    def charges_of(ref):
        parts = [split_dot(dot_nt, pair_of(ref, p), bdh[p], bdl[p]) for p in range(leaves // 2)]
        return jnp.concatenate(parts, axis=1)

    def row_sum(first, second):
        total = first[0] * second[0]
        for l in range(1, leaves):
            total = total + first[l] * second[l]
        return jnp.sum(total, axis=1, keepdims=True)

    def post_message(slot, root, norm, product):
        half = (128 - rank) // 2
        gather[slot, me, :, 0:rank] = root
        gather[slot, me, :, rank : rank + half] = jnp.broadcast_to(norm, (columns, half))
        gather[slot, me, :, rank + half : 128] = jnp.broadcast_to(product, (columns, half))
        broadcast(slot)

    def sums_of(slot):
        total = gather[slot, 0]
        for d in range(1, devices):
            total = total + gather[slot, d]
        half = (128 - rank) // 2
        return total[:, rank : rank + 1], total[:, rank + half : rank + half + 1]

    def potential_of(slot):
        group = min(devices, 16)

        def add(step, total):
            for i in range(group):
                x = step * group + i
                d = flipped(me, x, bits)
                total = total + dot_nn(gather[slot, d][:, 0:rank], t_ref[x], HIGH)
            return total

        return lax.fori_loop(0, devices // group, add, jnp.zeros((columns, rank), F32))

    bdh[...] = jnp.zeros_like(bdh)
    bdl[...] = jnp.zeros_like(bdl)
    for l in range(leaves):
        odd = l % 2
        rows, cols = slice(odd * rank, (odd + 1) * rank), slice(odd * n, (odd + 1) * n)
        bdh[l // 2, rows, cols], bdl[l // 2, rows, cols] = split2(basis_ref[l])
        res[l] = rhs_ref[:, l * n : (l + 1) * n]
    charge = charges_of(res)
    norm_local = row_sum(res, res)
    post_message(0, split_dot(dot_nn, charge, rh_ref[...], rl_ref[...]), norm_local, norm_local)

    sent[leaves * near] = jnp.zeros((columns, n), F32)

    def stack_right(x, row):
        hi, mid, lo = split3(x)
        nh, nm, nl = split3(-0.5 * jnp.sum(x * x, axis=0, keepdims=True))
        at = lax.broadcasted_iota(jnp.int32, (features, n), 0)
        extra = jnp.where(at < 3, 1.0, 0.0)
        for place, part in ((3, nh), (4, nm), (5, nl)):
            extra = jnp.where(at == place, part.astype(F32), extra)
        bj[row, 0:features, :] = hi
        bj[row, features : 2 * features, :] = mid
        bj[row, 2 * features : 3 * features, :] = lo
        bj[row, 3 * features : 4 * features, :] = extra.astype(BF16)

    def prepare(l, carry):
        at = pl.ds(pl.multiple_of(l * n, n), n)
        stack_right(pts_ref[:, at], l)
        stack_right(next_pts_ref[:, at], leaves + l)
        return carry

    lax.fori_loop(0, leaves, prepare, 0)

    def build(l, carry):
        x = pts_ref[:, pl.ds(pl.multiple_of(l * n, n), n)].T
        hi, mid, lo = split3(x)
        nh, nm, nl = split3(-0.5 * jnp.sum(x * x, axis=1, keepdims=True))
        at = lax.broadcasted_iota(jnp.int32, (n, features), 1)
        extra = jnp.where((at >= 3) & (at < 6), 1.0, 0.0)
        for place, part in ((0, nh), (1, nm), (2, nl)):
            extra = jnp.where(at == place, part.astype(F32), extra)
        left = jnp.concatenate([hi, hi, mid, mid, hi, lo, extra.astype(BF16)], axis=1)
        for k in range(slots):
            m = idx_ref[l, k]
            rh = bj[m, 0:features, :]
            rm = bj[m, features : 2 * features, :]
            rl = bj[m, 2 * features : 3 * features, :]
            rx = bj[m, 3 * features : 4 * features, :]
            right = jnp.concatenate([rh, rm, rh, rm, rl, rh, rx], axis=0)
            block = jnp.exp(dot_nn(left, right) * (1.0 / features)) * wt_ref[l, k]
            hi_part, lo_part = split2(block)
            kh[l * slots + k] = hi_part
            kl[l * slots + k] = lo_part
        return carry

    lax.fori_loop(0, leaves, build, 0)

    halo = None
    step = ratio = norm_now = None
    for sweep in range(ITERS):
        slot = sweep % 2
        field = res if sweep == 0 else w

        def load_own(l, carry):
            vb[l, 0:columns, :], vb[l, columns : 2 * columns, :] = split2(field[l])
            return carry

        lax.fori_loop(0, leaves, load_own, 0)

        def transposed(l, carry):
            both = vb[l]
            high = both[0:columns]
            for k in range(near):
                first = dot_nn(both, kh[l * slots + k])
                second = dot_nn(high, kl[l * slots + k])
                sent[l * near + k] = first[0:columns] + first[columns:] + second
            return carry

        lax.fori_loop(0, leaves, transposed, 0)

        collect(slot)
        for c in range(leaves):
            own = jnp.zeros((columns, n), F32)
            beyond = jnp.zeros((columns, n), F32)
            for l in range(leaves):
                term = sent[inv_ref[l, c]]
                if l < c:
                    own = own + term
                else:
                    beyond = beyond + term
            img[c] = own + RIDGE * field[c]
            owed_out[c] = beyond
        owed = pltpu.make_async_remote_copy(
            src_ref=owed_out,
            dst_ref=owed_in,
            send_sem=o_send.at[sweep],
            recv_sem=o_recv.at[sweep],
            device_id={"pts": following},
            device_id_type=pl.DeviceIdType.MESH,
        )
        owed.start()

        potential = potential_of(slot)
        chi, clo = split2(charge)
        first = dot_nn(jnp.concatenate([chi, clo], axis=0), mh_ref[...])
        leaf_potential = first[0:columns] + first[columns:] + dot_nn(chi, ml_ref[...])
        leaf_potential = leaf_potential + split_dot(dot_nt, potential, rh_ref[...], rl_ref[...])
        for p in range(leaves // 2):
            x = leaf_potential[:, 2 * p * rank : 2 * (p + 1) * rank]
            far = split_dot(dot_nn, x, bdh[p], bdl[p])
            img[2 * p] = img[2 * p] + far[:, 0:n]
            img[2 * p + 1] = img[2 * p + 1] + far[:, n:]

        if halo is not None:
            halo.wait()
        for l in range(leaves):
            x = next_rhs_ref[:, l * n : (l + 1) * n] if sweep == 0 else halo_in[sweep - 1, l]
            vb[leaves + l, 0:columns, :], vb[leaves + l, columns : 2 * columns, :] = split2(x)

        def forward(l, carry):
            total = jnp.zeros((2 * columns, n), F32)
            low = jnp.zeros((columns, n), F32)
            for k in range(slots):
                both = vb[idx_ref[l, k]]
                total = total + dot_nt(both, kh[l * slots + k])
                low = low + dot_nt(both[0:columns], kl[l * slots + k])
            img[l] = img[l] + (total[0:columns] + total[columns:] + low)
            return carry

        lax.fori_loop(0, leaves, forward, 0)
        owed.wait()

        if sweep == 0:
            for l in range(leaves):
                w[l] = img[l] + owed_in[l]
        else:
            norm_next, product = sums_of(slot)
            if sweep == 1:
                step = norm_next / product
            else:
                ratio = norm_next / norm_now
                step = norm_next / (product - ratio * norm_next / step)
            norm_now = norm_next
            for l in range(leaves):
                at = slice(l * n, (l + 1) * n)
                d, a, z = res[l], w[l], img[l] + owed_in[l]
                if sweep > 1:
                    d = d + ratio * dirn[l]
                    a = a + ratio * along[l]
                    z = z + ratio * second_along[l]
                    sol_ref[:, at] = sol_ref[:, at] + step * d
                else:
                    sol_ref[:, at] = step * d
                dirn[l], along[l], second_along[l] = d, a, z
                res[l] = res[l] - step * a
                w[l] = w[l] - step * z

        slot = (sweep + 1) % 2
        root = jnp.zeros((columns, rank), F32)
        if sweep + 1 < ITERS:
            halo = pltpu.make_async_remote_copy(
                src_ref=w,
                dst_ref=halo_in.at[sweep],
                send_sem=h_send.at[sweep],
                recv_sem=h_recv.at[sweep],
                device_id={"pts": previous},
                device_id_type=pl.DeviceIdType.MESH,
            )
            halo.start()
            charge = charges_of(w)
            root = split_dot(dot_nn, charge, rh_ref[...], rl_ref[...])
        post_message(slot, root, row_sum(res, res), row_sum(res, w))

    slot = ITERS % 2
    collect(slot)
    norm_next, product = sums_of(slot)
    ratio = norm_next / norm_now
    step = norm_next / (product - ratio * norm_next / step)
    for l in range(leaves):
        at = slice(l * n, (l + 1) * n)
        sol_ref[:, at] = sol_ref[:, at] + step * (res[l] + ratio * dirn[l])
        out_ref[:, at] = res[l] - step * (w[l] + ratio * along[l])


def per_device(
    points,
    right_side,
    leaf_basis,
    local_transfer,
    local_skeleton,
    top_transfer,
    top_skeleton,
    node_slot,
    near_leaves,
):
    features = points.shape[0]
    leaves, rank, leaf_size = leaf_basis.shape
    columns = right_side.shape[0]
    near = near_leaves.shape[1]
    slots = near + 1
    devices = lax.axis_size("pts")
    position = lax.axis_index("pts")
    ring = [(source, (source - 1) % devices) for source in range(devices)]
    next_rhs = lax.ppermute(right_side, "pts", ring)
    next_points = lax.ppermute(points, "pts", ring)

    present = near_leaves >= 0
    partner = jnp.where(present, near_leaves - position * leaves, -1)
    ids = jnp.arange(leaves, dtype=jnp.int32)
    index = jnp.concatenate([jnp.maximum(partner, 0), ids[:, None]], axis=1)
    scale = 1.0 / math.sqrt(leaf_size)
    weight = jnp.concatenate([present, jnp.ones((leaves, 1), bool)], axis=1)
    weight = weight.astype(F32) * scale
    target = jnp.where(ids[:, None] < ids[None, :], ids[None, :], ids[None, :] + leaves)
    match = partner[:, None, :] == target[:, :, None]
    place = ids[:, None] * near + jnp.arange(near, dtype=jnp.int32)[None, :]
    inverse = jnp.min(jnp.where(match, place[:, None, :], leaves * near), axis=2)

    vmem = pl.BlockSpec(memory_space=pltpu.VMEM)
    smem = pl.BlockSpec(memory_space=pltpu.SMEM)
    inner = leaves * rank
    mh, ml, rh, rl, t = pl.pallas_call(
        functools.partial(tree_kernel, devices, leaves, rank),
        out_shape=(
            jax.ShapeDtypeStruct((inner, inner), BF16),
            jax.ShapeDtypeStruct((inner, inner), BF16),
            jax.ShapeDtypeStruct((inner, rank), BF16),
            jax.ShapeDtypeStruct((inner, rank), BF16),
            jax.ShapeDtypeStruct((devices, rank, rank), F32),
        ),
        in_specs=[smem] + [vmem] * 4,
        out_specs=(vmem,) * 5,
        scratch_shapes=[pltpu.VMEM((inner, rank), F32)],
        compiler_params=pltpu.CompilerParams(vmem_limit_bytes=48 * 1024 * 1024),
        cost_estimate=pl.CostEstimate(
            flops=20_000_000_000, bytes_accessed=20_000_000, transcendentals=0
        ),
        name="tree",
    )(
        node_slot,
        local_transfer.reshape(-1, rank),
        local_skeleton.reshape(-1, rank),
        top_transfer.reshape(-1, rank),
        top_skeleton.reshape(-1, rank),
    )

    field = (leaves, columns, leaf_size)
    width = leaves * leaf_size
    return pl.pallas_call(
        functools.partial(
            main_kernel, devices, leaves, rank, columns, leaf_size, features, slots
        ),
        out_shape=(jax.ShapeDtypeStruct((columns, width), F32),) * 2,
        in_specs=[smem] * 3 + [vmem] * 10,
        out_specs=(vmem,) * 2,
        scratch_shapes=[
            pltpu.VMEM((leaves * slots, leaf_size, leaf_size), BF16),
            pltpu.VMEM((leaves * slots, leaf_size, leaf_size), BF16),
            pltpu.VMEM((2 * leaves, 4 * features, leaf_size), BF16),
            pltpu.VMEM((leaves // 2, 2 * rank, 2 * leaf_size), BF16),
            pltpu.VMEM((leaves // 2, 2 * rank, 2 * leaf_size), BF16),
            pltpu.VMEM((2 * leaves, 2 * columns, leaf_size), BF16),
            pltpu.VMEM((leaves * near + 1, columns, leaf_size), F32),
            pltpu.VMEM(field, F32),
            pltpu.VMEM(field, F32),
            pltpu.VMEM(field, F32),
            pltpu.VMEM(field, F32),
            pltpu.VMEM(field, F32),
            pltpu.VMEM(field, F32),
            pltpu.VMEM((ITERS - 1,) + field, F32),
            pltpu.VMEM(field, F32),
            pltpu.VMEM(field, F32),
            pltpu.VMEM((2, devices, columns, 128), F32),
            pltpu.SemaphoreType.DMA((2,)),
            pltpu.SemaphoreType.DMA((2,)),
            pltpu.SemaphoreType.DMA((ITERS,)),
            pltpu.SemaphoreType.DMA((ITERS,)),
            pltpu.SemaphoreType.DMA((ITERS,)),
            pltpu.SemaphoreType.DMA((ITERS,)),
        ],
        compiler_params=pltpu.CompilerParams(
            collective_id=0, has_side_effects=True, vmem_limit_bytes=66 * 1000 * 1000
        ),
        name="gradients",
    )(index, weight, inverse, points, next_points, right_side, next_rhs, leaf_basis, mh, ml, rh, rl, t)


def solution(mesh):
    return jax.shard_map(
        per_device,
        mesh=mesh,
        in_specs=(
            P(None, ("groups", "pts")),
            P(None, ("groups", "pts")),
            P(("groups", "pts"), None, None),
            P(("groups", "pts"), None),
            P(("groups", "pts"), None),
            P("groups", None),
            P("groups", None),
            P("groups"),
            P(("groups", "pts"), None),
        ),
        out_specs=(P(None, ("groups", "pts")), P(None, ("groups", "pts"))),
        check_vma=False,
    )
```
